32 devices in a mesh: groups: 2 (over y), edge: 4 (over z), expert: 2 (over x), sys: 2 (over core).
Axes of the slice: x: 2, y: 2, z: 4, core: 2. Of those that a mesh axis runs over, the one named last changes fastest.
Arguments:
- edge_inputs: bfloat16 [8, 1792, 1280], P(('groups', 'expert', 'sys'), 'edge'), parts along dimension 0, may hold values from -6 to 6
- out_grad: bfloat16 [8, 1792, 1152], P(('groups', 'expert', 'sys'), 'edge'), parts along dimension 0, may hold values from -6 to 6
- expert_weights: bfloat16 [32, 1280, 1152], P('expert', 'edge'), may hold values from -0.15625 to 0.15625
- coef_table: float32 [16, 32], replicated, may hold values from 0.05 to 0.5
- system_kind: int32 [8], P('groups'), parts along dimension 0, may hold values from 0 to 15
- edge_counts: int32 [8], P('groups'), parts along dimension 0, may hold values from 896 to 1792, as said below
Outputs:
- input_grad: bfloat16 [8, 1792, 1280], P(('groups', 'expert', 'sys'), 'edge'), parts along dimension 0
- weight_grad: bfloat16 [64, 1280, 1152], P(('groups', 'expert'), 'edge'), parts along dimension 0
The draws below stay inside these ranges and needn't reach their ends.
There are 2 independent parts, one for each index of `groups`. The reference program is written for one: setup_inputs(seed, part) draws one part's arguments, and reference() takes and returns one part's arrays. A program takes and returns all parts, laid end to end along the dimension named above; an argument that names none is the same for every part. Nothing has to cross between parts.
Inputs may be any that keep to these rules, and one draw needn't show every extreme that they name: `edge_counts`: the live edges of a system are its first ones. One system has all 1792 slots live and another exactly half of them.
All inputs are finite; a program needn't handle non-finite values.
Results may differ from the reference program's by a relative error of at most 0.018.
Values may be sent and summed in bfloat16 or wider, within the bound.
A program may use at most 128 MiB of HBM per device.

```python
import math
import jax
import jax.numpy as jnp
from jax import lax

DIN = 1280
DOUT = 1152
EXPERTS = 32
KINDS = 16
EDGE_DEV = 448
SYSTEMS = 4
EDGES = 1792
N_EDGE = 4
N_EXPERT = 2


def draw_edge_counts(key, part):
    key_counts, key_order = jax.random.split(jax.random.fold_in(key, 7), 2)
    half_edges = EDGES // 2
    counts = jax.random.randint(key_counts, (SYSTEMS,), half_edges, EDGES + 1)
    order = jax.random.permutation(key_order, SYSTEMS)
    counts = jnp.where(order == 0, EDGES, counts)
    counts = jnp.where(order == 1, half_edges, counts)
    return counts.astype(jnp.int32)


def plant(result, stream_key, smallest, high):
    extent = result.shape
    spot = [jax.random.randint(jax.random.fold_in(stream_key, axis), (), 0, extent[axis]) for axis in range(len(extent))]
    result = result.at[tuple(spot)].set(smallest)
    longest = extent.index(max(extent))
    spot[longest] = (spot[longest] + 1) % extent[longest]
    return result.at[tuple(spot)].set(high)


def steps_of(stream_key, extent, shards, smallest, high):
    gain, own = 1.0, jax.random.fold_in(stream_key, 6)
    for dim, parts in shards:
        heights = jnp.exp(jax.random.uniform(jax.random.fold_in(own, dim), (parts,), jnp.float32, smallest / len(shards), high / len(shards)))
        gain = gain * jnp.repeat(heights, extent[dim] // parts).reshape([-1 if axis == dim else 1 for axis in range(len(extent))])
    return gain


def scatter_about(own_key, dims, scale, bound, cuts=(), kind=jnp.bfloat16):
    loudness = steps_of(own_key, dims, cuts, -0.22, 0.18) if cuts else 1.0
    result = jax.random.normal(own_key, dims, jnp.float32) * scale * loudness
    return jnp.minimum(jnp.maximum(result, -bound), bound).astype(kind)


def setup_inputs(seed: int = 0, part: int = 0) -> dict:
    splits = jax.random.split(jax.random.key(seed), 7)
    part_splits = jax.random.split(jax.random.fold_in(splits[6], part), 7)
    return {
        "edge_inputs": scatter_about(part_splits[0], (SYSTEMS, EDGES, DIN), 1.0, 6.0, ((0, 4), (1, 4))),
        "out_grad": scatter_about(part_splits[1], (SYSTEMS, EDGES, DOUT), 1.0, 6.0, ((0, 4), (1, 4))),
        "expert_weights": scatter_about(splits[2], (EXPERTS, DIN, DOUT), DIN ** -0.5, 0.15625, ((0, 2), (1, 4))),
        "coef_table": jnp.clip(jnp.exp(jax.random.uniform(splits[3], (KINDS, EXPERTS), jnp.float32, math.log(0.05), math.log(0.5))), 0.05, 0.5),
        "system_kind": plant(jax.random.randint(part_splits[4], (SYSTEMS,), 0, KINDS), jax.random.fold_in(part_splits[4], 1), 0, KINDS - 1).astype(jnp.int32),
        "edge_counts": draw_edge_counts(jax.random.fold_in(jax.random.fold_in(splits[6], part), 71), part),
    }


def reference(edge_inputs, out_grad, expert_weights, coef_table, system_kind, edge_counts):
    highest = lax.Precision.HIGHEST
    onehot = (system_kind[:, None] == jnp.arange(KINDS, dtype=jnp.int32)[None, :]).astype(jnp.float32)
    coeffs = jnp.dot(onehot, coef_table, precision=highest)
    live = jnp.arange(EDGES, dtype=jnp.int32)[None, :] < edge_counts[:, None]
    masked_grad = jnp.where(live[:, :, None], out_grad, jnp.zeros((), out_grad.dtype))
    per_block = EXPERTS // N_EXPERT
    weights_float = expert_weights.astype(jnp.float32).reshape(N_EXPERT, per_block, DIN, DOUT)

    def merge_one(row):
        scaled = row.reshape(N_EXPERT, per_block)
        partials = jnp.einsum('be,berd->brd', scaled, weights_float, precision=highest).astype(jnp.bfloat16)
        return lax.optimization_barrier(jnp.sum(partials.astype(jnp.float32), axis=0)).astype(jnp.bfloat16)
    merged = lax.map(merge_one, coeffs)

    def input_one(pair):
        grad_rows, merged_one = pair
        product = jnp.dot(grad_rows.astype(jnp.float32), merged_one.astype(jnp.float32).T, precision=highest)
        return product.astype(jnp.bfloat16)
    input_grad = lax.map(input_one, (masked_grad, merged))

    def system_one(pair):
        feat_rows, grad_rows = pair
        feat_blocks = feat_rows.astype(jnp.float32).reshape(N_EDGE, EDGE_DEV, DIN)
        grad_blocks = grad_rows.astype(jnp.float32).reshape(N_EDGE, EDGE_DEV, DOUT)
        block_grads = jnp.einsum('bnd,bnk->bdk', feat_blocks, grad_blocks, precision=highest).astype(jnp.bfloat16)
        return lax.optimization_barrier(jnp.sum(block_grads.astype(jnp.float32), axis=0)).astype(jnp.bfloat16)
    system_grads = lax.map(system_one, (edge_inputs, masked_grad))
    summed = jnp.einsum('se,sdk->edk', coeffs, system_grads.astype(jnp.float32), precision=highest)
    weight_grad = (summed * (1.0 / math.sqrt(EDGES))).astype(jnp.bfloat16)
    return (input_grad, weight_grad)
```

```python
import functools
import math

import jax
import jax.numpy as jnp
from jax import lax
from jax.experimental import pallas as pl
from jax.experimental.pallas import tpu as pltpu
from jax.sharding import PartitionSpec as P

MESH = pl.DeviceIdType.MESH
F32 = jnp.float32
BF16 = jnp.bfloat16


def split_rows(rows, most):
    sizes = [size for size in range(16, min(rows, most) + 1, 16) if rows % size == 0]
    return max(sizes) if sizes else rows


def lane_tile(width):
    return 256 if width % 256 == 0 else 128 if width % 128 == 0 else width


def exchange(
    n_edge, n_expert, n_sys, piece,
    kind_ref, count_ref, table_ref, feat_any, grad_any, weight_any,
    input_grad_ref, blocks_any,
    feat, grad, weight, prod, from_left, from_right, merged, part_out, part_in, final,
    load_sem, weight_sem, part_send, part_recv,
    sum_send, sum_recv, all_send, all_recv,
    peer_send, peer_recv, core_send, core_recv, own_sem,
):
    z = lax.axis_index("edge")
    x = lax.axis_index("expert")
    core = lax.axis_index("sys")
    own_system = x * n_sys + core
    rows = weight.shape[1]
    pieces = rows // piece
    n_exp = weight.shape[0]
    width = weight.shape[2]
    edge_rows, depth = feat.shape
    lanes = 384 if width % 384 == 0 else lane_tile(width)

    feat_copy = pltpu.make_async_copy(feat_any.at[0], feat, load_sem.at[0])
    grad_copy = pltpu.make_async_copy(grad_any.at[0], grad, load_sem.at[1])
    grad_copy.start()
    feat_copy.start()

    def weight_copy(c):
        span = pl.ds(c * piece, piece)
        return pltpu.make_async_copy(
            weight_any.at[:, span, :], weight.at[:, span, :], weight_sem.at[c]
        )

    for c in range(pieces):
        weight_copy(c).start()

    barrier = pltpu.get_barrier_semaphore()

    @pl.when(z > 0)
    def _():
        pl.semaphore_signal(barrier, inc=1, device_id={"edge": z - 1}, device_id_type=MESH)

    @pl.when(z < n_edge - 1)
    def _():
        pl.semaphore_signal(barrier, inc=1, device_id={"edge": z + 1}, device_id_type=MESH)

    for t in range(n_expert):
        @pl.when(x != t)
        def _():
            pl.semaphore_signal(barrier, inc=1, device_id={"expert": t}, device_id_type=MESH)
    for t in range(n_sys):
        @pl.when(core != t)
        def _():
            pl.semaphore_signal(barrier, inc=1, device_id={"sys": t}, device_id_type=MESH)
    neighbours = jnp.where(z > 0, 1, 0) + jnp.where(z < n_edge - 1, 1, 0)
    pl.semaphore_wait(barrier, neighbours + (n_expert - 1) + (n_sys - 1))

    grad_copy.wait()
    live = count_ref[own_system] - z * edge_rows
    mask_rows = split_rows(edge_rows, 64)

    def mask_step(i, carry):
        at = pl.multiple_of(i * mask_rows, mask_rows)
        span = pl.ds(at, mask_rows)
        place = at + lax.broadcasted_iota(jnp.int32, (mask_rows, width), 0)
        values = grad[span, :].astype(F32)
        grad[span, :] = jnp.where(place < live, values, 0.0).astype(BF16)
        return carry

    lax.fori_loop(0, edge_rows // mask_rows, mask_step, 0)
    feat_copy.wait()

    tile = lane_tile(depth)

    def product_step(i, carry):
        span = pl.ds(pl.multiple_of(i * tile, tile), tile)
        prod[span, :] = lax.dot_general(
            feat[:, span], grad[...], (((0,), (0,)), ((), ())), preferred_element_type=F32
        ).astype(BF16)
        return carry

    lax.fori_loop(0, depth // tile, product_step, 0)

    def block(j, c):
        start = j * rows + c * piece
        return pl.ds(start if isinstance(start, int) else pl.multiple_of(start, 16), piece)

    def sum_copy(way, j, c):
        landing = from_left if way == 0 else from_right
        target = z + 1 if way == 0 else z - 1
        sem = (way * n_edge + j) * pieces + c
        return pltpu.make_async_remote_copy(
            src_ref=prod.at[block(j, c)],
            dst_ref=landing.at[block(j, c)],
            send_sem=sum_send.at[sem],
            recv_sem=sum_recv.at[sem],
            device_id={"edge": target},
            device_id_type=MESH,
        )

    def sum_step(m, c):
        high, low = n_edge - 1 - m, m

        @pl.when(z < high)
        def _():
            @pl.when(z > 0)
            def _():
                sum_copy(0, high, c).wait_recv()
                span = block(high, c)
                prod[span, :] = (
                    prod[span, :].astype(F32) + from_left[span, :].astype(F32)
                ).astype(BF16)

            sum_copy(0, high, c).start()

        @pl.when(z > low)
        def _():
            @pl.when(z < n_edge - 1)
            def _():
                sum_copy(1, low, c).wait_recv()
                span = block(low, c)
                prod[span, :] = (
                    prod[span, :].astype(F32) + from_right[span, :].astype(F32)
                ).astype(BF16)

            sum_copy(1, low, c).start()

    def peer_copy(t, source, c):
        span = pl.ds(c * piece, piece)
        return pltpu.make_async_remote_copy(
            src_ref=final.at[span],
            dst_ref=blocks_any.at[source * n_sys + core, span],
            send_sem=peer_send.at[t * pieces + c],
            recv_sem=peer_recv.at[source * pieces + c],
            device_id={"expert": t},
            device_id_type=MESH,
        )

    def core_copy(t, source, from_core, c, own):
        span = pl.ds(c * piece, piece)
        place = blocks_any.at[source * n_sys + from_core, span]
        return pltpu.make_async_remote_copy(
            src_ref=final.at[span] if own else place,
            dst_ref=place,
            send_sem=core_send.at[(t * n_expert + source) * pieces + c],
            recv_sem=core_recv.at[(from_core * n_expert + source) * pieces + c],
            device_id={"sys": t},
            device_id_type=MESH,
        )

    def own_copy(c):
        span = pl.ds(c * piece, piece)
        return pltpu.make_async_copy(
            final.at[span], blocks_any.at[own_system, span], own_sem.at[c]
        )

    def final_step(c):
        @pl.when(z > 0)
        def _():
            sum_copy(0, z, c).wait_recv()

        @pl.when(z < n_edge - 1)
        def _():
            sum_copy(1, z, c).wait_recv()

        span = block(z, c)
        out = pl.ds(c * piece, piece)

        @pl.when(z == 0)
        def _():
            final[out, :] = (
                prod[span, :].astype(F32) + from_right[span, :].astype(F32)
            ).astype(BF16)

        @pl.when(z == n_edge - 1)
        def _():
            final[out, :] = (
                prod[span, :].astype(F32) + from_left[span, :].astype(F32)
            ).astype(BF16)

        @pl.when(jnp.logical_and(z > 0, z < n_edge - 1))
        def _():
            final[out, :] = (
                prod[span, :].astype(F32)
                + from_left[span, :].astype(F32)
                + from_right[span, :].astype(F32)
            ).astype(BF16)

        for t in range(n_expert):
            @pl.when(x != t)
            def _():
                peer_copy(t, x, c).start()
        for t in range(n_sys):
            @pl.when(core != t)
            def _():
                core_copy(t, x, core, c, True).start()
        own_copy(c).start()

    def part_copy(t, source, c):
        span = pl.ds(c * piece, piece)
        return pltpu.make_async_remote_copy(
            src_ref=part_out.at[t, span],
            dst_ref=part_in.at[source, span],
            send_sem=part_send.at[t * pieces + c],
            recv_sem=part_recv.at[source * pieces + c],
            device_id={"expert": t},
            device_id_type=MESH,
        )

    kinds = [kind_ref[t * n_sys + core] for t in range(n_expert)]
    gains = [
        [table_ref[kinds[t], x * n_exp + e] for e in range(n_exp)] for t in range(n_expert)
    ]

    def part_step(c):
        weight_copy(c).wait()

        def row_step(i, carry):
            span = pl.ds(pl.multiple_of(c * piece + i * 16, 16), 16)
            for col in range(0, width, lanes):
                cols = slice(col, col + lanes)
                sums = [None] * n_expert
                for e in range(n_exp):
                    value = weight[e, span, cols].astype(F32)
                    for t in range(n_expert):
                        term = value * gains[t][e]
                        sums[t] = term if sums[t] is None else sums[t] + term
                for t in range(n_expert):
                    part_out[t, span, cols] = sums[t].astype(BF16)
            return carry

        lax.fori_loop(0, piece // 16, row_step, 0)
        for t in range(n_expert):
            @pl.when(x != t)
            def _():
                part_copy(t, x, c).start()

    def all_copy(way, j, c):
        target = z + 1 if way == 0 else z - 1
        sem = (way * n_edge + j) * pieces + c
        return pltpu.make_async_remote_copy(
            src_ref=merged.at[block(j, c)],
            dst_ref=merged.at[block(j, c)],
            send_sem=all_send.at[sem],
            recv_sem=all_recv.at[sem],
            device_id={"edge": target},
            device_id_type=MESH,
        )

    def all_first(c):
        span = pl.ds(c * piece, piece)
        for b in range(n_expert):
            @pl.when(x != b)
            def _():
                part_copy(b, b, c).wait_recv()
        total = part_out[x, span, :].astype(F32)
        for step in range(1, n_expert):
            total += part_in[lax.rem(x + step, n_expert), span, :].astype(F32)
        merged[block(z, c), :] = total.astype(BF16)

        @pl.when(z < n_edge - 1)
        def _():
            all_copy(0, z, c).start()

        @pl.when(z > 0)
        def _():
            all_copy(1, z, c).start()

    def all_step(m, c):
        @pl.when(z - m >= 0)
        def _():
            all_copy(0, z - m, c).wait_recv()

            @pl.when(z < n_edge - 1)
            def _():
                all_copy(0, z - m, c).start()

        @pl.when(z + m < n_edge)
        def _():
            all_copy(1, z + m, c).wait_recv()

            @pl.when(z > 0)
            def _():
                all_copy(1, z + m, c).start()

    for m in range(n_edge):
        if m == 0:
            @pl.when(jnp.logical_or(z == 0, z == n_edge - 1))
            def _():
                for c in range(pieces):
                    @pl.when(z == 0)
                    def _():
                        sum_copy(0, n_edge - 1, c).start()

                    @pl.when(z == n_edge - 1)
                    def _():
                        sum_copy(1, 0, c).start()

            for c in range(pieces):
                part_step(c)
            for c in range(pieces):
                @pl.when(jnp.logical_and(z > 0, z < n_edge - 1))
                def _():
                    sum_step(0, c)
        elif m < n_edge - 1:
            for c in range(pieces):
                sum_step(m, c)
        for c in range(pieces):
            if m == 0:
                all_first(c)
            else:
                all_step(m, c)
        if m == max(n_edge - 2, 0):
            for c in range(pieces):
                final_step(c)

    for c in range(pieces):
        for b in range(n_expert):
            @pl.when(x != b)
            def _():
                peer_copy(b, b, c).wait_recv()
                for t in range(n_sys):
                    @pl.when(core != t)
                    def _():
                        core_copy(t, b, core, c, False).start()

    def input_step(i, carry):
        span = pl.ds(pl.multiple_of(i * tile, tile), tile)
        input_grad_ref[0, :, span] = lax.dot_general(
            grad[...], merged[span, :], (((1,), (1,)), ((), ())), preferred_element_type=F32
        ).astype(BF16)
        return carry

    lax.fori_loop(0, depth // tile, input_step, 0)

    for c in range(pieces):
        own_copy(c).wait()
        for t in range(n_expert):
            @pl.when(x != t)
            def _():
                peer_copy(t, x, c).wait_send()
                part_copy(t, x, c).wait_send()
        for t in range(n_sys):
            @pl.when(core != t)
            def _():
                for b in range(n_expert):
                    core_copy(t, b, t, c, False).wait_recv()
                    core_copy(t, b, core, c, False).wait_send()
        for j in range(n_edge):
            @pl.when(z < j)
            def _():
                sum_copy(0, j, c).wait_send()

            @pl.when(z > j)
            def _():
                sum_copy(1, j, c).wait_send()

            @pl.when(jnp.logical_and(j <= z, z < n_edge - 1))
            def _():
                all_copy(0, j, c).wait_send()

            @pl.when(jnp.logical_and(j >= z, z > 0))
            def _():
                all_copy(1, j, c).wait_send()


def expand(n_sys, scale, kind_ref, table_ref, block_ref, out_ref, gains):
    systems, rows, width = block_ref.shape
    n_exp = out_ref.shape[0]
    x = lax.axis_index("expert")
    depth = systems * rows

    @pl.when(pl.program_id(0) == 0)
    def _():
        lane = lax.broadcasted_iota(jnp.int32, (rows, depth), 1)
        row = lax.broadcasted_iota(jnp.int32, (rows, depth), 0)
        for e in range(n_exp):
            values = jnp.zeros((rows, depth), F32)
            for s in range(systems):
                gain = table_ref[kind_ref[s], x * n_exp + e] * scale
                values = jnp.where(lane == row + s * rows, gain, values)
            gains[pl.ds(e * rows, rows), :] = values.astype(BF16)

    stacked = block_ref[...].reshape(depth, width)
    group = max(1, min(n_exp, 256 // rows))
    while n_exp % group:
        group -= 1

    def step(i, carry):
        at = pl.multiple_of(i * group * rows, 16)
        result = jnp.dot(
            gains[pl.ds(at, group * rows), :], stacked, preferred_element_type=F32
        )
        out_ref[pl.ds(i * group, group)] = result.astype(BF16).reshape(group, rows, width)
        return carry

    lax.fori_loop(0, n_exp // group, step, 0)


def body(edge_inputs, out_grad, expert_weights, coef_table, system_kind, edge_counts):
    n_edge = lax.axis_size("edge")
    n_expert = lax.axis_size("expert")
    n_sys = lax.axis_size("sys")
    systems = system_kind.shape[0]
    n_exp, rows, width = expert_weights.shape
    edge_rows, depth = edge_inputs.shape[1:]
    piece = split_rows(rows, 80)
    pieces = rows // piece
    dma = lambda count: pltpu.SemaphoreType.DMA((count,))
    smem = pl.BlockSpec(memory_space=pltpu.SMEM)
    anywhere = pl.BlockSpec(memory_space=pl.ANY)
    vmem = pl.BlockSpec(memory_space=pltpu.VMEM)
    input_grad, blocks = pl.pallas_call(
        functools.partial(exchange, n_edge, n_expert, n_sys, piece),
        out_shape=(
            jax.ShapeDtypeStruct((1, edge_rows, depth), BF16),
            jax.ShapeDtypeStruct((systems, rows, width), BF16),
        ),
        in_specs=[smem, smem, smem, anywhere, anywhere, anywhere],
        out_specs=(vmem, anywhere),
        scratch_shapes=[
            pltpu.VMEM((edge_rows, depth), BF16),
            pltpu.VMEM((edge_rows, width), BF16),
            pltpu.VMEM((n_exp, rows, width), BF16),
            pltpu.VMEM((depth, width), BF16),
            pltpu.VMEM((depth, width), BF16),
            pltpu.VMEM((depth, width), BF16),
            pltpu.VMEM((depth, width), BF16),
            pltpu.VMEM((n_expert, rows, width), BF16),
            pltpu.VMEM((n_expert, rows, width), BF16),
            pltpu.VMEM((rows, width), BF16),
            dma(2),
            dma(pieces),
            dma(n_expert * pieces),
            dma(n_expert * pieces),
            dma(2 * n_edge * pieces),
            dma(2 * n_edge * pieces),
            dma(2 * n_edge * pieces),
            dma(2 * n_edge * pieces),
            dma(n_expert * pieces),
            dma(n_expert * pieces),
            dma(n_sys * n_expert * pieces),
            dma(n_sys * n_expert * pieces),
            dma(pieces),
        ],
        compiler_params=pltpu.CompilerParams(
            collective_id=0, has_side_effects=True, vmem_limit_bytes=50 * 2**20
        ),
        name="exchange",
    )(system_kind, edge_counts, coef_table, edge_inputs, out_grad, expert_weights)

    block_rows = split_rows(rows, max(16, 256 // systems))
    scale = 1.0 / math.sqrt(edge_rows * n_edge)
    weight_grad = pl.pallas_call(
        functools.partial(expand, n_sys, scale),
        grid=(rows // block_rows,),
        out_shape=jax.ShapeDtypeStruct((n_exp, rows, width), BF16),
        in_specs=[smem, smem, pl.BlockSpec((systems, block_rows, width), lambda i: (0, i, 0))],
        out_specs=pl.BlockSpec((n_exp, block_rows, width), lambda i: (0, i, 0)),
        scratch_shapes=[pltpu.VMEM((n_exp * block_rows, systems * block_rows), BF16)],
        compiler_params=pltpu.CompilerParams(vmem_limit_bytes=40 * 2**20),
        name="expand",
    )(system_kind, coef_table, blocks)
    return (input_grad, weight_grad)


def solution(mesh):
    return jax.shard_map(
        body,
        mesh=mesh,
        in_specs=(
            P(("groups", "expert", "sys"), "edge", None),
            P(("groups", "expert", "sys"), "edge", None),
            P("expert", "edge", None),
            P(),
            P("groups"),
            P("groups"),
        ),
        out_specs=(
            P(("groups", "expert", "sys"), "edge", None),
            P(("groups", "expert"), "edge", None),
        ),
        check_vma=False,
    )
```

```python
import functools
import math

import jax
import jax.numpy as jnp
from jax import lax
from jax.experimental import pallas as pl
from jax.experimental.pallas import tpu as pltpu
from jax.sharding import PartitionSpec as P

MESH = pl.DeviceIdType.MESH
F32 = jnp.float32
BF16 = jnp.bfloat16


def split_rows(rows, most):
    sizes = [size for size in range(16, min(rows, most) + 1, 16) if rows % size == 0]
    return max(sizes) if sizes else rows


def lane_tile(width):
    return 256 if width % 256 == 0 else 128 if width % 128 == 0 else width


def exchange(
    n_edge, n_expert, n_sys, piece,
    kind_any, count_any, table_any, feat_any, grad_any, weight_any,
    input_grad_ref, blocks_any,
    kind_ref, count_ref, table_ref,
    feat, grad, weight, prod, from_left, from_right, merged, part_out, part_in, final,
    load_sem, weight_sem, part_send, part_recv,
    sum_send, sum_recv, all_send, all_recv,
    peer_send, peer_recv, core_send, core_recv, own_sem,
):
    z = lax.axis_index("edge")
    x = lax.axis_index("expert")
    core = lax.axis_index("sys")
    own_system = x * n_sys + core
    rows = weight.shape[1]
    pieces = rows // piece
    n_exp = weight.shape[0]
    width = weight.shape[2]
    edge_rows, depth = feat.shape
    lanes = 384 if width % 384 == 0 else lane_tile(width)

    feat_copy = pltpu.make_async_copy(feat_any.at[0], feat, load_sem.at[0])
    grad_copy = pltpu.make_async_copy(grad_any.at[0], grad, load_sem.at[1])
    small_copies = [
        pltpu.make_async_copy(source, target, load_sem.at[2 + i])
        for i, (source, target) in enumerate(
            ((count_any, count_ref), (kind_any, kind_ref), (table_any, table_ref))
        )
    ]
    grad_copy.start()
    for copy in small_copies:
        copy.start()
    feat_copy.start()

    def weight_copy(c):
        span = pl.ds(c * piece, piece)
        return pltpu.make_async_copy(
            weight_any.at[:, span, :], weight.at[:, span, :], weight_sem.at[c]
        )

    for c in range(pieces):
        weight_copy(c).start()

    barrier = pltpu.get_barrier_semaphore()

    @pl.when(z > 0)
    def _():
        pl.semaphore_signal(barrier, inc=1, device_id={"edge": z - 1}, device_id_type=MESH)

    @pl.when(z < n_edge - 1)
    def _():
        pl.semaphore_signal(barrier, inc=1, device_id={"edge": z + 1}, device_id_type=MESH)

    for t in range(n_expert):
        @pl.when(x != t)
        def _():
            pl.semaphore_signal(barrier, inc=1, device_id={"expert": t}, device_id_type=MESH)
    for t in range(n_sys):
        @pl.when(core != t)
        def _():
            pl.semaphore_signal(barrier, inc=1, device_id={"sys": t}, device_id_type=MESH)
    neighbours = jnp.where(z > 0, 1, 0) + jnp.where(z < n_edge - 1, 1, 0)
    pl.semaphore_wait(barrier, neighbours + (n_expert - 1) + (n_sys - 1))

    for copy in small_copies:
        copy.wait()
    grad_copy.wait()
    live = count_ref[own_system] - z * edge_rows
    mask_rows = split_rows(edge_rows, 64)

    def mask_step(i, carry):
        at = pl.multiple_of(i * mask_rows, mask_rows)
        span = pl.ds(at, mask_rows)
        place = at + lax.broadcasted_iota(jnp.int32, (mask_rows, width), 0)
        values = grad[span, :].astype(F32)
        grad[span, :] = jnp.where(place < live, values, 0.0).astype(BF16)
        return carry

    lax.fori_loop(0, edge_rows // mask_rows, mask_step, 0)
    feat_copy.wait()

    tile = lane_tile(depth)

    lower = z < n_edge // 2
    tiles = depth // tile

    def product_step(i, carry):
        at = jnp.where(lower, tiles - 1 - i, i)
        span = pl.ds(pl.multiple_of(at * tile, tile), tile)
        prod[span, :] = lax.dot_general(
            feat[:, span], grad[...], (((0,), (0,)), ((), ())), preferred_element_type=F32
        ).astype(BF16)
        return carry

    ahead = pl.cdiv(rows, tile)
    lax.fori_loop(0, ahead, product_step, 0)

    def block(j, c):
        start = j * rows + c * piece
        return pl.ds(start if isinstance(start, int) else pl.multiple_of(start, 16), piece)

    def sum_copy(way, j, c):
        landing = from_left if way == 0 else from_right
        target = z + 1 if way == 0 else z - 1
        sem = (way * n_edge + j) * pieces + c
        return pltpu.make_async_remote_copy(
            src_ref=prod.at[block(j, c)],
            dst_ref=landing.at[block(j, c)],
            send_sem=sum_send.at[sem],
            recv_sem=sum_recv.at[sem],
            device_id={"edge": target},
            device_id_type=MESH,
        )

    def sum_step(m, c):
        high, low = n_edge - 1 - m, m

        @pl.when(z < high)
        def _():
            @pl.when(z > 0)
            def _():
                sum_copy(0, high, c).wait_recv()
                span = block(high, c)
                prod[span, :] = (
                    prod[span, :].astype(F32) + from_left[span, :].astype(F32)
                ).astype(BF16)

            sum_copy(0, high, c).start()

        @pl.when(z > low)
        def _():
            @pl.when(z < n_edge - 1)
            def _():
                sum_copy(1, low, c).wait_recv()
                span = block(low, c)
                prod[span, :] = (
                    prod[span, :].astype(F32) + from_right[span, :].astype(F32)
                ).astype(BF16)

            sum_copy(1, low, c).start()

    def peer_copy(t, source, c):
        span = pl.ds(c * piece, piece)
        return pltpu.make_async_remote_copy(
            src_ref=final.at[span],
            dst_ref=blocks_any.at[source * n_sys + core, span],
            send_sem=peer_send.at[t * pieces + c],
            recv_sem=peer_recv.at[source * pieces + c],
            device_id={"expert": t},
            device_id_type=MESH,
        )

    def core_copy(t, source, from_core, c, own):
        span = pl.ds(c * piece, piece)
        place = blocks_any.at[source * n_sys + from_core, span]
        return pltpu.make_async_remote_copy(
            src_ref=final.at[span] if own else place,
            dst_ref=place,
            send_sem=core_send.at[(t * n_expert + source) * pieces + c],
            recv_sem=core_recv.at[(from_core * n_expert + source) * pieces + c],
            device_id={"sys": t},
            device_id_type=MESH,
        )

    def own_copy(c):
        span = pl.ds(c * piece, piece)
        return pltpu.make_async_copy(
            final.at[span], blocks_any.at[own_system, span], own_sem.at[c]
        )

    def final_step(c):
        @pl.when(z > 0)
        def _():
            sum_copy(0, z, c).wait_recv()

        @pl.when(z < n_edge - 1)
        def _():
            sum_copy(1, z, c).wait_recv()

        span = block(z, c)
        out = pl.ds(c * piece, piece)

        @pl.when(z == 0)
        def _():
            final[out, :] = (
                prod[span, :].astype(F32) + from_right[span, :].astype(F32)
            ).astype(BF16)

        @pl.when(z == n_edge - 1)
        def _():
            final[out, :] = (
                prod[span, :].astype(F32) + from_left[span, :].astype(F32)
            ).astype(BF16)

        @pl.when(jnp.logical_and(z > 0, z < n_edge - 1))
        def _():
            final[out, :] = (
                prod[span, :].astype(F32)
                + from_left[span, :].astype(F32)
                + from_right[span, :].astype(F32)
            ).astype(BF16)

        for t in range(n_expert):
            @pl.when(x != t)
            def _():
                peer_copy(t, x, c).start()
        for t in range(n_sys):
            @pl.when(core != t)
            def _():
                core_copy(t, x, core, c, True).start()
        own_copy(c).start()

    def part_copy(t, source, c):
        span = pl.ds(c * piece, piece)
        return pltpu.make_async_remote_copy(
            src_ref=part_out.at[t, span],
            dst_ref=part_in.at[source, span],
            send_sem=part_send.at[t * pieces + c],
            recv_sem=part_recv.at[source * pieces + c],
            device_id={"expert": t},
            device_id_type=MESH,
        )

    kinds = [kind_ref[t * n_sys + core] for t in range(n_expert)]
    gains = [
        [table_ref[kinds[t], x * n_exp + e] for e in range(n_exp)] for t in range(n_expert)
    ]

    def part_step(c):
        weight_copy(c).wait()

        def row_step(i, carry):
            span = pl.ds(pl.multiple_of(c * piece + i * 16, 16), 16)
            for col in range(0, width, lanes):
                cols = slice(col, col + lanes)
                sums = [None] * n_expert
                for e in range(n_exp):
                    value = weight[e, span, cols].astype(F32)
                    for t in range(n_expert):
                        term = value * gains[t][e]
                        sums[t] = term if sums[t] is None else sums[t] + term
                for t in range(n_expert):
                    part_out[t, span, cols] = sums[t].astype(BF16)
            return carry

        lax.fori_loop(0, piece // 16, row_step, 0)
        for t in range(n_expert):
            @pl.when(x != t)
            def _():
                part_copy(t, x, c).start()

    def all_copy(way, j, c):
        target = z + 1 if way == 0 else z - 1
        sem = (way * n_edge + j) * pieces + c
        return pltpu.make_async_remote_copy(
            src_ref=merged.at[block(j, c)],
            dst_ref=merged.at[block(j, c)],
            send_sem=all_send.at[sem],
            recv_sem=all_recv.at[sem],
            device_id={"edge": target},
            device_id_type=MESH,
        )

    def own_rows(c):
        span = pl.ds(c * piece, piece)
        for b in range(n_expert):
            @pl.when(x != b)
            def _():
                part_copy(b, b, c).wait_recv()
        total = part_out[x, span, :].astype(F32)
        for step in range(1, n_expert):
            total += part_in[lax.rem(x + step, n_expert), span, :].astype(F32)
        merged[block(z, c), :] = total.astype(BF16)

    def own_send(way, c):
        @pl.when(z < n_edge - 1 if way == 0 else z > 0)
        def _():
            all_copy(way, z, c).start()

    def all_step(way, m, c):
        j = z - m if way == 0 else z + m

        @pl.when(j >= 0 if way == 0 else j < n_edge)
        def _():
            all_copy(way, j, c).wait_recv()

            @pl.when(z < n_edge - 1 if way == 0 else z > 0)
            def _():
                all_copy(way, j, c).start()

    def by_half(function, far, *args):
        @pl.when(lower)
        def _():
            function(1 if far else 0, *args)

        @pl.when(jnp.logical_not(lower))
        def _():
            function(0 if far else 1, *args)

    def peer_step(c):
        for b in range(n_expert):
            @pl.when(x != b)
            def _():
                peer_copy(b, b, c).wait_recv()
                for t in range(n_sys):
                    @pl.when(core != t)
                    def _():
                        core_copy(t, b, core, c, False).start()

    def end_sums(m):
        for c in range(pieces):
            @pl.when(z == 0)
            def _():
                sum_copy(0, n_edge - 1 - m, c).start()

            @pl.when(z == n_edge - 1)
            def _():
                sum_copy(1, m, c).start()

    inside = jnp.logical_and(z > 0, z < n_edge - 1)

    def inside_sums(m, c):
        @pl.when(inside)
        def _():
            sum_step(m, c)

    end_sums(0)
    lax.fori_loop(ahead, tiles, product_step, 0)
    for m in range(1, n_edge - 1):
        end_sums(m)

    for c in range(pieces):
        part_step(c)
        if c > 0:
            inside_sums(0, c - 1)
    inside_sums(0, pieces - 1)
    for c in range(pieces):
        own_rows(c)
        by_half(own_send, True, c)
    for c in range(pieces):
        if n_edge > 2:
            inside_sums(1, c)
        by_half(own_send, False, c)
    for m in range(2, n_edge - 1):
        for c in range(pieces):
            inside_sums(m, c)
    for c in range(pieces):
        final_step(c)
        by_half(all_step, True, 1, c)
    for m in range(1, n_edge):
        for c in range(pieces):
            by_half(all_step, False, m, c)
            if m + 1 < n_edge:
                by_half(all_step, True, m + 1, c)
            if m == 1:
                peer_step(c)

    def input_step(i, carry):
        span = pl.ds(pl.multiple_of(i * tile, tile), tile)
        input_grad_ref[0, :, span] = lax.dot_general(
            grad[...], merged[span, :], (((1,), (1,)), ((), ())), preferred_element_type=F32
        ).astype(BF16)
        return carry

    lax.fori_loop(0, depth // tile, input_step, 0)

    for c in range(pieces):
        own_copy(c).wait()
        for t in range(n_expert):
            @pl.when(x != t)
            def _():
                peer_copy(t, x, c).wait_send()
                part_copy(t, x, c).wait_send()
        for t in range(n_sys):
            @pl.when(core != t)
            def _():
                for b in range(n_expert):
                    core_copy(t, b, t, c, False).wait_recv()
                    core_copy(t, b, core, c, False).wait_send()
        for j in range(n_edge):
            @pl.when(z < j)
            def _():
                sum_copy(0, j, c).wait_send()

            @pl.when(z > j)
            def _():
                sum_copy(1, j, c).wait_send()

            @pl.when(jnp.logical_and(j <= z, z < n_edge - 1))
            def _():
                all_copy(0, j, c).wait_send()

            @pl.when(jnp.logical_and(j >= z, z > 0))
            def _():
                all_copy(1, j, c).wait_send()


def expand(n_sys, scale, kind_ref, table_ref, block_ref, out_ref, gains):
    systems, rows, width = block_ref.shape
    n_exp = out_ref.shape[0]
    x = lax.axis_index("expert")
    depth = systems * rows

    @pl.when(pl.program_id(0) == 0)
    def _():
        lane = lax.broadcasted_iota(jnp.int32, (rows, depth), 1)
        row = lax.broadcasted_iota(jnp.int32, (rows, depth), 0)
        for e in range(n_exp):
            values = jnp.zeros((rows, depth), F32)
            for s in range(systems):
                gain = table_ref[kind_ref[s], x * n_exp + e] * scale
                values = jnp.where(lane == row + s * rows, gain, values)
            gains[pl.ds(e * rows, rows), :] = values.astype(BF16)

    stacked = block_ref[...].reshape(depth, width)
    group = max(1, min(n_exp, 256 // rows))
    while n_exp % group:
        group -= 1

    for i in range(n_exp // group):
        at = i * group * rows
        result = jnp.dot(
            gains[pl.ds(at, group * rows), :], stacked, preferred_element_type=F32
        )
        out_ref[pl.ds(i * group, group)] = result.astype(BF16).reshape(group, rows, width)


def body(edge_inputs, out_grad, expert_weights, coef_table, system_kind, edge_counts):
    n_edge = lax.axis_size("edge")
    n_expert = lax.axis_size("expert")
    n_sys = lax.axis_size("sys")
    systems = system_kind.shape[0]
    n_exp, rows, width = expert_weights.shape
    edge_rows, depth = edge_inputs.shape[1:]
    piece = split_rows(rows, 80)
    pieces = rows // piece
    dma = lambda count: pltpu.SemaphoreType.DMA((count,))
    smem = pl.BlockSpec(memory_space=pltpu.SMEM)
    anywhere = pl.BlockSpec(memory_space=pl.ANY)
    vmem = pl.BlockSpec(memory_space=pltpu.VMEM)
    input_grad, blocks = pl.pallas_call(
        functools.partial(exchange, n_edge, n_expert, n_sys, piece),
        out_shape=(
            jax.ShapeDtypeStruct((1, edge_rows, depth), BF16),
            jax.ShapeDtypeStruct((systems, rows, width), BF16),
        ),
        in_specs=[anywhere] * 6,
        out_specs=(vmem, anywhere),
        scratch_shapes=[
            pltpu.SMEM(system_kind.shape, jnp.int32),
            pltpu.SMEM(edge_counts.shape, jnp.int32),
            pltpu.SMEM(coef_table.shape, F32),
            pltpu.VMEM((edge_rows, depth), BF16),
            pltpu.VMEM((edge_rows, width), BF16),
            pltpu.VMEM((n_exp, rows, width), BF16),
            pltpu.VMEM((depth, width), BF16),
            pltpu.VMEM((depth, width), BF16),
            pltpu.VMEM((depth, width), BF16),
            pltpu.VMEM((depth, width), BF16),
            pltpu.VMEM((n_expert, rows, width), BF16),
            pltpu.VMEM((n_expert, rows, width), BF16),
            pltpu.VMEM((rows, width), BF16),
            dma(5),
            dma(pieces),
            dma(n_expert * pieces),
            dma(n_expert * pieces),
            dma(2 * n_edge * pieces),
            dma(2 * n_edge * pieces),
            dma(2 * n_edge * pieces),
            dma(2 * n_edge * pieces),
            dma(n_expert * pieces),
            dma(n_expert * pieces),
            dma(n_sys * n_expert * pieces),
            dma(n_sys * n_expert * pieces),
            dma(pieces),
        ],
        compiler_params=pltpu.CompilerParams(
            collective_id=0, has_side_effects=True, vmem_limit_bytes=60 * 2**20
        ),
        name="exchange",
    )(system_kind, edge_counts, coef_table, edge_inputs, out_grad, expert_weights)

    block_rows = split_rows(rows, max(16, 256 // systems))
    scale = 1.0 / math.sqrt(edge_rows * n_edge)
    weight_grad = pl.pallas_call(
        functools.partial(expand, n_sys, scale),
        grid=(rows // block_rows,),
        out_shape=jax.ShapeDtypeStruct((n_exp, rows, width), BF16),
        in_specs=[smem, smem, pl.BlockSpec((systems, block_rows, width), lambda i: (0, i, 0))],
        out_specs=pl.BlockSpec((n_exp, block_rows, width), lambda i: (0, i, 0)),
        scratch_shapes=[pltpu.VMEM((n_exp * block_rows, systems * block_rows), BF16)],
        compiler_params=pltpu.CompilerParams(vmem_limit_bytes=60 * 2**20),
        name="expand",
    )(system_kind, coef_table, blocks)
    return (input_grad, weight_grad)


def solution(mesh):
    return jax.shard_map(
        body,
        mesh=mesh,
        in_specs=(
            P(("groups", "expert", "sys"), "edge", None),
            P(("groups", "expert", "sys"), "edge", None),
            P("expert", "edge", None),
            P(),
            P("groups"),
            P("groups"),
        ),
        out_specs=(
            P(("groups", "expert", "sys"), "edge", None),
            P(("groups", "expert"), "edge", None),
        ),
        check_vma=False,
    )
```

```python
import functools
import math

import jax
import jax.numpy as jnp
from jax import lax
from jax.experimental import pallas as pl
from jax.experimental.pallas import tpu as pltpu
from jax.sharding import PartitionSpec as P

MESH = pl.DeviceIdType.MESH
F32 = jnp.float32
BF16 = jnp.bfloat16


def split_rows(rows, most):
    sizes = [size for size in range(16, min(rows, most) + 1, 16) if rows % size == 0]
    return max(sizes) if sizes else rows


def lane_tile(width):
    return 256 if width % 256 == 0 else 128 if width % 128 == 0 else width


def exchange(
    n_edge, n_expert, n_sys, piece,
    kind_any, count_any, table_any, feat_any, grad_any, weight_any,
    input_grad_ref, blocks_any,
    kind_ref, count_ref, table_ref,
    feat, grad, weight, prod, from_left, from_right, merged, part_out, part_in, final,
    load_sem, weight_sem, part_send, part_recv,
    sum_send, sum_recv, all_send, all_recv,
    peer_send, peer_recv, core_send, core_recv, own_sem,
):
    z = lax.axis_index("edge")
    x = lax.axis_index("expert")
    core = lax.axis_index("sys")
    own_system = x * n_sys + core
    rows = weight.shape[1]
    pieces = rows // piece
    n_exp = weight.shape[0]
    width = weight.shape[2]
    edge_rows, depth = feat.shape
    lanes = 384 if width % 384 == 0 else lane_tile(width)

    feat_copy = pltpu.make_async_copy(feat_any.at[0], feat, load_sem.at[0])
    grad_copy = pltpu.make_async_copy(grad_any.at[0], grad, load_sem.at[1])
    small_copies = [
        pltpu.make_async_copy(source, target, load_sem.at[2 + i])
        for i, (source, target) in enumerate(
            ((count_any, count_ref), (kind_any, kind_ref), (table_any, table_ref))
        )
    ]
    grad_copy.start()
    for copy in small_copies:
        copy.start()
    feat_copy.start()

    def weight_copy(c):
        span = pl.ds(c * piece, piece)
        return pltpu.make_async_copy(
            weight_any.at[:, span, :], weight.at[:, span, :], weight_sem.at[c]
        )

    for c in range(pieces):
        weight_copy(c).start()

    barrier = pltpu.get_barrier_semaphore()

    @pl.when(z > 0)
    def _():
        pl.semaphore_signal(barrier, inc=1, device_id={"edge": z - 1}, device_id_type=MESH)

    @pl.when(z < n_edge - 1)
    def _():
        pl.semaphore_signal(barrier, inc=1, device_id={"edge": z + 1}, device_id_type=MESH)

    for t in range(n_expert):
        @pl.when(x != t)
        def _():
            pl.semaphore_signal(barrier, inc=1, device_id={"expert": t}, device_id_type=MESH)
    for t in range(n_sys):
        @pl.when(core != t)
        def _():
            pl.semaphore_signal(barrier, inc=1, device_id={"sys": t}, device_id_type=MESH)
    neighbours = jnp.where(z > 0, 1, 0) + jnp.where(z < n_edge - 1, 1, 0)
    pl.semaphore_wait(barrier, neighbours + (n_expert - 1) + (n_sys - 1))

    for copy in small_copies:
        copy.wait()
    grad_copy.wait()
    live = count_ref[own_system] - z * edge_rows
    mask_rows = split_rows(edge_rows, 64)

    def mask_step(i, carry):
        at = pl.multiple_of(i * mask_rows, mask_rows)
        span = pl.ds(at, mask_rows)
        place = at + lax.broadcasted_iota(jnp.int32, (mask_rows, width), 0)
        values = grad[span, :].astype(F32)
        grad[span, :] = jnp.where(place < live, values, 0.0).astype(BF16)
        return carry

    lax.fori_loop(0, edge_rows // mask_rows, mask_step, 0)
    feat_copy.wait()

    tile = lane_tile(depth)

    lower = z < n_edge // 2
    tiles = depth // tile

    def product_step(i, carry):
        at = jnp.where(lower, tiles - 1 - i, i)
        span = pl.ds(pl.multiple_of(at * tile, tile), tile)
        prod[span, :] = lax.dot_general(
            feat[:, span], grad[...], (((0,), (0,)), ((), ())), preferred_element_type=F32
        ).astype(BF16)
        return carry

    ahead = pl.cdiv(rows, tile)
    lax.fori_loop(0, ahead, product_step, 0)

    def block(j, c):
        start = j * rows + c * piece
        return pl.ds(start if isinstance(start, int) else pl.multiple_of(start, 16), piece)

    def sum_copy(way, j, c):
        landing = from_left if way == 0 else from_right
        target = z + 1 if way == 0 else z - 1
        sem = (way * n_edge + j) * pieces + c
        return pltpu.make_async_remote_copy(
            src_ref=prod.at[block(j, c)],
            dst_ref=landing.at[block(j, c)],
            send_sem=sum_send.at[sem],
            recv_sem=sum_recv.at[sem],
            device_id={"edge": target},
            device_id_type=MESH,
        )

    def sum_step(m, c):
        high, low = n_edge - 1 - m, m

        @pl.when(z < high)
        def _():
            @pl.when(z > 0)
            def _():
                sum_copy(0, high, c).wait_recv()
                span = block(high, c)
                prod[span, :] = (
                    prod[span, :].astype(F32) + from_left[span, :].astype(F32)
                ).astype(BF16)

            sum_copy(0, high, c).start()

        @pl.when(z > low)
        def _():
            @pl.when(z < n_edge - 1)
            def _():
                sum_copy(1, low, c).wait_recv()
                span = block(low, c)
                prod[span, :] = (
                    prod[span, :].astype(F32) + from_right[span, :].astype(F32)
                ).astype(BF16)

            sum_copy(1, low, c).start()

    def peer_copy(t, source, c):
        span = pl.ds(c * piece, piece)
        return pltpu.make_async_remote_copy(
            src_ref=final.at[span],
            dst_ref=blocks_any.at[source * n_sys + core, span],
            send_sem=peer_send.at[t * pieces + c],
            recv_sem=peer_recv.at[source * pieces + c],
            device_id={"expert": t},
            device_id_type=MESH,
        )

    def core_copy(t, source, from_core, c, own):
        span = pl.ds(c * piece, piece)
        place = blocks_any.at[source * n_sys + from_core, span]
        return pltpu.make_async_remote_copy(
            src_ref=final.at[span] if own else place,
            dst_ref=place,
            send_sem=core_send.at[(t * n_expert + source) * pieces + c],
            recv_sem=core_recv.at[(from_core * n_expert + source) * pieces + c],
            device_id={"sys": t},
            device_id_type=MESH,
        )

    def own_copy(c):
        span = pl.ds(c * piece, piece)
        return pltpu.make_async_copy(
            final.at[span], blocks_any.at[own_system, span], own_sem.at[c]
        )

    def final_step(c):
        @pl.when(z > 0)
        def _():
            sum_copy(0, z, c).wait_recv()

        @pl.when(z < n_edge - 1)
        def _():
            sum_copy(1, z, c).wait_recv()

        span = block(z, c)
        out = pl.ds(c * piece, piece)

        @pl.when(z == 0)
        def _():
            final[out, :] = (
                prod[span, :].astype(F32) + from_right[span, :].astype(F32)
            ).astype(BF16)

        @pl.when(z == n_edge - 1)
        def _():
            final[out, :] = (
                prod[span, :].astype(F32) + from_left[span, :].astype(F32)
            ).astype(BF16)

        @pl.when(jnp.logical_and(z > 0, z < n_edge - 1))
        def _():
            final[out, :] = (
                prod[span, :].astype(F32)
                + from_left[span, :].astype(F32)
                + from_right[span, :].astype(F32)
            ).astype(BF16)

        for t in range(n_expert):
            @pl.when(x != t)
            def _():
                peer_copy(t, x, c).start()
        for t in range(n_sys):
            @pl.when(core != t)
            def _():
                core_copy(t, x, core, c, True).start()
        own_copy(c).start()

    def part_copy(t, source, c):
        span = pl.ds(c * piece, piece)
        return pltpu.make_async_remote_copy(
            src_ref=part_out.at[t, span],
            dst_ref=part_in.at[source, span],
            send_sem=part_send.at[t * pieces + c],
            recv_sem=part_recv.at[source * pieces + c],
            device_id={"expert": t},
            device_id_type=MESH,
        )

    kinds = [kind_ref[t * n_sys + core] for t in range(n_expert)]
    gains = [
        [table_ref[kinds[t], x * n_exp + e] for e in range(n_exp)] for t in range(n_expert)
    ]

    def part_step(c):
        weight_copy(c).wait()

        def row_step(i, carry):
            span = pl.ds(pl.multiple_of(c * piece + i * 16, 16), 16)
            for col in range(0, width, lanes):
                cols = slice(col, col + lanes)
                sums = [None] * n_expert
                for e in range(n_exp):
                    value = weight[e, span, cols].astype(F32)
                    for t in range(n_expert):
                        term = value * gains[t][e]
                        sums[t] = term if sums[t] is None else sums[t] + term
                for t in range(n_expert):
                    part_out[t, span, cols] = sums[t].astype(BF16)
            return carry

        lax.fori_loop(0, piece // 16, row_step, 0)
        for t in range(n_expert):
            @pl.when(x != t)
            def _():
                part_copy(t, x, c).start()

    def all_copy(way, j, c):
        target = z + 1 if way == 0 else z - 1
        sem = (way * n_edge + j) * pieces + c
        return pltpu.make_async_remote_copy(
            src_ref=merged.at[block(j, c)],
            dst_ref=merged.at[block(j, c)],
            send_sem=all_send.at[sem],
            recv_sem=all_recv.at[sem],
            device_id={"edge": target},
            device_id_type=MESH,
        )

    def own_rows(c):
        span = pl.ds(c * piece, piece)
        for b in range(n_expert):
            @pl.when(x != b)
            def _():
                part_copy(b, b, c).wait_recv()
        total = part_out[x, span, :].astype(F32)
        for step in range(1, n_expert):
            total += part_in[lax.rem(x + step, n_expert), span, :].astype(F32)
        merged[block(z, c), :] = total.astype(BF16)

    def own_send(way, c):
        @pl.when(z < n_edge - 1 if way == 0 else z > 0)
        def _():
            all_copy(way, z, c).start()

    def all_step(way, m, c):
        j = z - m if way == 0 else z + m

        @pl.when(j >= 0 if way == 0 else j < n_edge)
        def _():
            all_copy(way, j, c).wait_recv()

            @pl.when(z < n_edge - 1 if way == 0 else z > 0)
            def _():
                all_copy(way, j, c).start()

    def by_half(function, far, *args):
        @pl.when(lower)
        def _():
            function(1 if far else 0, *args)

        @pl.when(jnp.logical_not(lower))
        def _():
            function(0 if far else 1, *args)

    def peer_step(c):
        for b in range(n_expert):
            @pl.when(x != b)
            def _():
                peer_copy(b, b, c).wait_recv()
                for t in range(n_sys):
                    @pl.when(core != t)
                    def _():
                        core_copy(t, b, core, c, False).start()

    def end_sums(m):
        for c in range(pieces):
            @pl.when(z == 0)
            def _():
                sum_copy(0, n_edge - 1 - m, c).start()

            @pl.when(z == n_edge - 1)
            def _():
                sum_copy(1, m, c).start()

    inside = jnp.logical_and(z > 0, z < n_edge - 1)

    def inside_sums(m, c):
        @pl.when(inside)
        def _():
            sum_step(m, c)

    end_sums(0)
    lax.fori_loop(ahead, tiles, product_step, 0)
    for m in range(1, n_edge - 1):
        end_sums(m)

    for c in range(pieces):
        part_step(c)
        if c > 0:
            inside_sums(0, c - 1)
    inside_sums(0, pieces - 1)
    for c in range(pieces):
        own_rows(c)
        by_half(own_send, True, c)
    for c in range(pieces):
        if n_edge > 2:
            inside_sums(1, c)
        by_half(own_send, False, c)
    for m in range(2, n_edge - 1):
        for c in range(pieces):
            inside_sums(m, c)
    for c in range(pieces):
        final_step(c)
        by_half(all_step, True, 1, c)
    for m in range(1, n_edge):
        for c in range(pieces):
            by_half(all_step, False, m, c)
            if m + 1 < n_edge:
                by_half(all_step, True, m + 1, c)
            if m == 1:
                peer_step(c)

    def input_step(i, carry):
        span = pl.ds(pl.multiple_of(i * tile, tile), tile)
        input_grad_ref[0, :, span] = lax.dot_general(
            grad[...], merged[span, :], (((1,), (1,)), ((), ())), preferred_element_type=F32
        ).astype(BF16)
        return carry

    lax.fori_loop(0, depth // tile, input_step, 0)

    for c in range(pieces):
        own_copy(c).wait()
        for t in range(n_expert):
            @pl.when(x != t)
            def _():
                peer_copy(t, x, c).wait_send()
                part_copy(t, x, c).wait_send()
        for t in range(n_sys):
            @pl.when(core != t)
            def _():
                for b in range(n_expert):
                    core_copy(t, b, t, c, False).wait_recv()
                    core_copy(t, b, core, c, False).wait_send()
        for j in range(n_edge):
            @pl.when(z < j)
            def _():
                sum_copy(0, j, c).wait_send()

            @pl.when(z > j)
            def _():
                sum_copy(1, j, c).wait_send()

            @pl.when(jnp.logical_and(j <= z, z < n_edge - 1))
            def _():
                all_copy(0, j, c).wait_send()

            @pl.when(jnp.logical_and(j >= z, z > 0))
            def _():
                all_copy(1, j, c).wait_send()


def expand(n_sys, scale, kind_ref, table_ref, block_ref, out_ref, gains):
    systems, rows, width = block_ref.shape
    n_exp = out_ref.shape[0]
    x = lax.axis_index("expert")
    depth = systems * rows

    @pl.when(pl.program_id(0) == 0)
    def _():
        lane = lax.broadcasted_iota(jnp.int32, (rows, depth), 1)
        row = lax.broadcasted_iota(jnp.int32, (rows, depth), 0)
        for e in range(n_exp):
            values = jnp.zeros((rows, depth), F32)
            for s in range(systems):
                gain = table_ref[kind_ref[s], x * n_exp + e] * scale
                values = jnp.where(lane == row + s * rows, gain, values)
            gains[pl.ds(e * rows, rows), :] = values.astype(BF16)

    stacked = block_ref[...].reshape(depth, width)
    group = max(1, min(n_exp, 256 // rows))
    while n_exp % group:
        group -= 1

    for i in range(n_exp // group):
        at = i * group * rows
        result = jnp.dot(
            gains[pl.ds(at, group * rows), :], stacked, preferred_element_type=F32
        )
        out_ref[pl.ds(i * group, group)] = result.astype(BF16).reshape(group, rows, width)


def body(edge_inputs, out_grad, expert_weights, coef_table, system_kind, edge_counts):
    n_edge = lax.axis_size("edge")
    n_expert = lax.axis_size("expert")
    n_sys = lax.axis_size("sys")
    systems = system_kind.shape[0]
    n_exp, rows, width = expert_weights.shape
    edge_rows, depth = edge_inputs.shape[1:]
    piece = split_rows(rows, 160)
    pieces = rows // piece
    dma = lambda count: pltpu.SemaphoreType.DMA((count,))
    smem = pl.BlockSpec(memory_space=pltpu.SMEM)
    anywhere = pl.BlockSpec(memory_space=pl.ANY)
    vmem = pl.BlockSpec(memory_space=pltpu.VMEM)
    input_grad, blocks = pl.pallas_call(
        functools.partial(exchange, n_edge, n_expert, n_sys, piece),
        out_shape=(
            jax.ShapeDtypeStruct((1, edge_rows, depth), BF16),
            jax.ShapeDtypeStruct((systems, rows, width), BF16),
        ),
        in_specs=[anywhere] * 6,
        out_specs=(vmem, anywhere),
        scratch_shapes=[
            pltpu.SMEM(system_kind.shape, jnp.int32),
            pltpu.SMEM(edge_counts.shape, jnp.int32),
            pltpu.SMEM(coef_table.shape, F32),
            pltpu.VMEM((edge_rows, depth), BF16),
            pltpu.VMEM((edge_rows, width), BF16),
            pltpu.VMEM((n_exp, rows, width), BF16),
            pltpu.VMEM((depth, width), BF16),
            pltpu.VMEM((depth, width), BF16),
            pltpu.VMEM((depth, width), BF16),
            pltpu.VMEM((depth, width), BF16),
            pltpu.VMEM((n_expert, rows, width), BF16),
            pltpu.VMEM((n_expert, rows, width), BF16),
            pltpu.VMEM((rows, width), BF16),
            dma(5),
            dma(pieces),
            dma(n_expert * pieces),
            dma(n_expert * pieces),
            dma(2 * n_edge * pieces),
            dma(2 * n_edge * pieces),
            dma(2 * n_edge * pieces),
            dma(2 * n_edge * pieces),
            dma(n_expert * pieces),
            dma(n_expert * pieces),
            dma(n_sys * n_expert * pieces),
            dma(n_sys * n_expert * pieces),
            dma(pieces),
        ],
        compiler_params=pltpu.CompilerParams(
            collective_id=0, has_side_effects=True, vmem_limit_bytes=60 * 2**20
        ),
        name="exchange",
    )(system_kind, edge_counts, coef_table, edge_inputs, out_grad, expert_weights)

    block_rows = split_rows(rows, max(16, 256 // systems))
    scale = 1.0 / math.sqrt(edge_rows * n_edge)
    weight_grad = pl.pallas_call(
        functools.partial(expand, n_sys, scale),
        grid=(rows // block_rows,),
        out_shape=jax.ShapeDtypeStruct((n_exp, rows, width), BF16),
        in_specs=[smem, smem, pl.BlockSpec((systems, block_rows, width), lambda i: (0, i, 0))],
        out_specs=pl.BlockSpec((n_exp, block_rows, width), lambda i: (0, i, 0)),
        scratch_shapes=[pltpu.VMEM((n_exp * block_rows, systems * block_rows), BF16)],
        compiler_params=pltpu.CompilerParams(vmem_limit_bytes=60 * 2**20),
        name="expand",
    )(system_kind, coef_table, blocks)
    return (input_grad, weight_grad)


def solution(mesh):
    return jax.shard_map(
        body,
        mesh=mesh,
        in_specs=(
            P(("groups", "expert", "sys"), "edge", None),
            P(("groups", "expert", "sys"), "edge", None),
            P("expert", "edge", None),
            P(),
            P("groups"),
            P("groups"),
        ),
        out_specs=(
            P(("groups", "expert", "sys"), "edge", None),
            P(("groups", "expert"), "edge", None),
        ),
        check_vma=False,
    )
```
